128 devices in a mesh: row: 8 (over x_lo, z), col: 4 (over x_hi, core), rep: 4 (over y).
Axes of the slice: x: 4 (x_hi: 2, x_lo: 2; x = x_hi * 2 + x_lo), y: 4, z: 4, core: 2. Of those that a mesh axis runs over, the one named last changes fastest.
Arguments:
- p_matrix: bfloat16 [49152, 16384], P('row', ('col', 'rep')), may hold values from -6 to 6
- s_matrix: bfloat16 [16384, 2048], P(('col', 'rep')), may hold values from -0.09375 to 0.09375
- p_pattern: int32 [384, 128], P('row', ('col', 'rep')), may hold values 0 or 1
- s_pattern: int32 [128, 16], P(('col', 'rep')), may hold values 0 or 1
- c_input: float32 [49152, 2048], P('row', ('col', 'rep')), may hold values from -6 to 6
- step: int32 [1], replicated, may hold values from 0 to 4095
Outputs:
- c_output: float32 [49152, 2048], P('row', ('col', 'rep'))
The draws below stay inside these ranges and needn't reach their ends.
All inputs are finite; a program needn't handle non-finite values. No bound on the sum of `p_pattern` or of `s_pattern` on one device may be relied on, other than what follows from the above.
Results may differ from the reference program's by a relative error of at most 0.005.
Values may be sent and summed in bfloat16 or wider, within the bound.
A program may use at most 128 MiB of HBM per device.

```python
import jax
import jax.numpy as jnp
from jax import lax

BLOCK = 128
RB_DEV = 48
KB_DEV = 8
M = 49152
K = 16384
NC = 2048
MB = 384
KB = 128
NCB = 16
N_ROW = 8
N_COL = 4
N_REP = 4


def set_ends(array, stream_key, smallest, high):
    shape = array.shape
    index_at = [jax.random.randint(jax.random.fold_in(stream_key, axis), (), 0, shape[axis]) for axis in range(len(shape))]
    array = array.at[tuple(index_at)].set(smallest)
    longest = shape.index(max(shape))
    index_at[longest] = (index_at[longest] + 1) % shape[longest]
    return array.at[tuple(index_at)].set(high)


def block_scale(own_key, shape, split, least, largest):
    level, own = 1.0, jax.random.fold_in(own_key, 6)
    for dim, blocks in split:
        draws = jnp.exp(jax.random.uniform(jax.random.fold_in(own, dim), (blocks,), jnp.float32, least / len(split), largest / len(split)))
        level = level * jnp.repeat(draws, shape[dim] // blocks).reshape([-1 if axis == dim else 1 for axis in range(len(shape))])
    return level


def bell_draw(key, dims, spread, most, split=(), held_as=jnp.bfloat16):
    level = block_scale(key, dims, split, -0.22, 0.18) if split else 1.0
    result = jax.random.normal(key, dims, jnp.float32) * spread * level
    return jnp.minimum(jnp.maximum(result, -most), most).astype(held_as)


def setup_inputs(seed: int = 0) -> dict:
    seeds = jax.random.split(jax.random.key(seed), 7)
    p_matrix = bell_draw(seeds[0], (M, K), 1.0, 6.0, ((0, 8), (1, 16)))
    s_matrix = bell_draw(seeds[1], (K, NC), (K // N_COL) ** -0.5, 0.09375, ((0, 16),))
    p_pattern = set_ends((jax.random.randint(seeds[2], (MB, KB), 0, 2) < 1).astype(jnp.int32), jax.random.fold_in(seeds[2], 1), 0, 1)
    s_pattern = set_ends((jax.random.randint(seeds[3], (KB, NCB), 0, 2) < 1).astype(jnp.int32), jax.random.fold_in(seeds[3], 1), 0, 1)
    c_input = bell_draw(seeds[4], (M, NC), 1.0, 6.0, ((0, 8), (1, 16)), jnp.float32)
    step = jax.random.randint(seeds[5], (1,), 0, 1024 * N_COL).astype(jnp.int32)
    return dict(p_matrix=p_matrix, s_matrix=s_matrix, p_pattern=p_pattern, s_pattern=s_pattern, c_input=c_input, step=step)


def masked(matrix, pattern):
    row_blocks, col_blocks = pattern.shape
    shaped = matrix.reshape(row_blocks, BLOCK, col_blocks, BLOCK)
    shaped = shaped * pattern[:, None, :, None].astype(matrix.dtype)
    return shaped.reshape(row_blocks * BLOCK, col_blocks * BLOCK)


def reference(p_matrix, s_matrix, p_pattern, s_pattern, c_input, step):
    row_span = RB_DEV * BLOCK
    piece_width = KB_DEV * BLOCK
    col_group = NC // N_COL
    rows_out = []
    for group_row in range(N_ROW):
        cols_out = []
        for group_col in range(N_COL):
            panel_index = (group_row + group_col + step[0]) % N_COL
            running = jnp.zeros((row_span, col_group), jnp.float32)
            for layer in range(N_REP):
                offset = ((panel_index * N_REP + layer) * piece_width).astype(jnp.int32)
                block_offset = ((panel_index * N_REP + layer) * KB_DEV).astype(jnp.int32)
                p_part = lax.dynamic_slice(p_matrix, (jnp.int32(group_row * row_span), offset), (row_span, piece_width))
                p_mask = lax.dynamic_slice(p_pattern, (jnp.int32(group_row * RB_DEV), block_offset), (RB_DEV, KB_DEV))
                s_part = lax.dynamic_slice(s_matrix, (offset, jnp.int32(group_col * col_group)), (piece_width, col_group))
                s_mask = lax.dynamic_slice(s_pattern, (block_offset, jnp.int32(group_col * col_group // BLOCK)), (KB_DEV, col_group // BLOCK))
                left = masked(p_part, p_mask).astype(jnp.float32)
                right = masked(s_part, s_mask).astype(jnp.float32)
                layer_term = jnp.dot(left, right, precision=lax.Precision.HIGHEST, preferred_element_type=jnp.float32)
                layer_term = lax.optimization_barrier(layer_term.astype(jnp.bfloat16))
                running = running + layer_term.astype(jnp.float32)
            earlier = c_input[group_row * row_span:(group_row + 1) * row_span, group_col * col_group:(group_col + 1) * col_group]
            cols_out.append(earlier + running)
        rows_out.append(jnp.concatenate(cols_out, axis=1))
    return jnp.concatenate(rows_out, axis=0)
```

```python
import functools

import jax
import jax.numpy as jnp
from jax import lax
from jax.experimental import pallas as pl
from jax.experimental.pallas import tpu as pltpu
from jax.sharding import PartitionSpec as P

BLOCK = 128
CHUNK = 512
HALF = CHUNK // 2
LAG_ADD, LAG_SUM, LAG_OUT = 2, 4, 6
MESH = pl.DeviceIdType.MESH


def kernel(
    shift, chunks, p_pat, s_pat, p_hbm, s_hbm, c_hbm, o_hbm,
    p_v, s_v, c_v, o_v, own, wait_lo, wait_hi, far_s, lo_s, hi_s, move_s,
    far_r, lo_r, hi_r, move_r,
    p_sem, s_sem, c_sem, o_sem, far_ss, far_rs, lo_ss, lo_rs, hi_ss, hi_rs, move_ss, move_rs,
):
    row, col, rep = lax.axis_index("row"), lax.axis_index("col"), lax.axis_index("rep")
    distance = lax.rem(row + shift, 4)
    target = lax.rem(col + 4 - distance, 4)
    origin = lax.rem(col + distance, 4)
    group = target
    up, down = {"rep": lax.rem(rep + 1, 4)}, {"rep": lax.rem(rep + 3, 4)}
    moves = distance != 0

    barrier = pltpu.get_barrier_semaphore()
    for neighbour in (up, down):
        pl.semaphore_signal(barrier, inc=1, device_id=neighbour, device_id_type=MESH)

    @pl.when(moves)
    def _():
        pl.semaphore_signal(barrier, inc=1, device_id={"col": target}, device_id_type=MESH)
        pl.semaphore_signal(barrier, inc=1, device_id={"col": origin}, device_id_type=MESH)

    def s_load(k):
        at = pl.multiple_of((group * 4 + lax.rem(rep + k, 4)) * BLOCK, BLOCK)
        return pltpu.make_async_copy(
            s_hbm.at[:, pl.ds(at, BLOCK)], s_v.at[:, pl.ds(k * BLOCK, BLOCK)], s_sem.at[k]
        )

    def p_load(i):
        return pltpu.make_async_copy(p_hbm.at[pl.ds(i * CHUNK, CHUNK)], p_v.at[i], p_sem.at[i])

    def c_load():
        return pltpu.make_async_copy(c_hbm, c_v, c_sem)

    def o_store(i):
        return pltpu.make_async_copy(o_v.at[i], o_hbm.at[pl.ds(i * CHUNK, CHUNK)], o_sem.at[i])

    def remote(source, target_ref, send, receive, device):
        return pltpu.make_async_remote_copy(
            src_ref=source, dst_ref=target_ref, send_sem=send, recv_sem=receive,
            device_id=device, device_id_type=MESH,
        )

    def far_down(i):
        return remote(far_s.at[i, 0], far_r.at[i, 0], far_ss.at[i, 0], far_rs.at[i, 0], down)

    def far_up(i):
        return remote(far_s.at[i, 1], far_r.at[i, 1], far_ss.at[i, 1], far_rs.at[i, 1], up)

    def near_down(i):
        return remote(lo_s.at[i], hi_r.at[i], lo_ss.at[i], hi_rs.at[i], down)

    def near_up(i):
        return remote(hi_s.at[i], lo_r.at[i], hi_ss.at[i], lo_rs.at[i], up)

    def move(i):
        return remote(move_s.at[i], move_r.at[i], move_ss.at[i], move_rs.at[i], {"col": target})

    for k in range(4):
        s_load(k).start()
    p_load(0).start()
    p_load(1).start()
    c_load().start()

    def start_p(i, carry):
        p_load(i).start()
        return carry

    lax.fori_loop(2, chunks, start_p, 0)

    for k in range(4):
        s_load(k).wait()
        for b in range(8):
            rows, columns = pl.ds(b * BLOCK, BLOCK), pl.ds(k * BLOCK, BLOCK)
            keep = s_pat[b, group * 4 + lax.rem(rep + k, 4)].astype(jnp.float32).astype(jnp.bfloat16)
            s_v[rows, columns] = s_v[rows, columns] * keep

    def produce(i):
        p_load(i).wait()
        for a in range(CHUNK // BLOCK):
            for b in range(8):
                rows, columns = pl.ds(a * BLOCK, BLOCK), pl.ds(b * BLOCK, BLOCK)
                keep = p_pat[i * (CHUNK // BLOCK) + a, b].astype(jnp.float32).astype(jnp.bfloat16)
                p_v[i, rows, columns] = p_v[i, rows, columns] * keep
        term = jnp.dot(p_v[i], s_v[...], preferred_element_type=jnp.float32)
        far = term[:, 2 * BLOCK:3 * BLOCK].astype(jnp.bfloat16)
        far_s[i, 0] = far[:HALF]
        far_s[i, 1] = far[HALF:]
        own[i] = term[:, :BLOCK]
        hi_s[i, :HALF] = term[:HALF, BLOCK:2 * BLOCK].astype(jnp.bfloat16)
        wait_hi[i] = term[HALF:, BLOCK:2 * BLOCK]
        wait_lo[i] = term[:HALF, 3 * BLOCK:]
        lo_s[i, HALF:] = term[HALF:, 3 * BLOCK:].astype(jnp.bfloat16)

    def send_far(i):
        far_down(i).start()
        far_up(i).start()

    def add(i):
        far_down(i).wait_recv()
        lo_s[i, :HALF] = (wait_lo[i] + far_r[i, 0].astype(jnp.float32)).astype(jnp.bfloat16)
        near_down(i).start()
        far_up(i).wait_recv()
        hi_s[i, HALF:] = (wait_hi[i] + far_r[i, 1].astype(jnp.float32)).astype(jnp.bfloat16)
        near_up(i).start()

    def total(i):
        near_down(i).wait_recv()
        near_up(i).wait_recv()
        summed = own[i] + hi_r[i].astype(jnp.float32) + lo_r[i].astype(jnp.float32)
        summed = summed.astype(jnp.bfloat16)

        @pl.when(moves)
        def _():
            move_s[i] = summed
            move(i).start()

        @pl.when(jnp.logical_not(moves))
        def _():
            move_r[i] = summed

    def finish(i):
        @pl.when(moves)
        def _():
            move(i).wait_recv()

        at = pl.ds(i * CHUNK, CHUNK)
        o_v[i] = c_v[at] + move_r[i].astype(jnp.float32)
        o_store(i).start()

    produce(0)

    @pl.when(moves)
    def _():
        pl.semaphore_wait(barrier, 4)

    @pl.when(jnp.logical_not(moves))
    def _():
        pl.semaphore_wait(barrier, 2)

    send_far(0)
    c_load().wait()

    def body(t, carry):
        @pl.when(t < chunks)
        def _():
            produce(t)
            send_far(t)

        @pl.when(jnp.logical_and(t >= LAG_ADD, t < chunks + LAG_ADD))
        def _():
            add(t - LAG_ADD)

        @pl.when(jnp.logical_and(t >= LAG_SUM, t < chunks + LAG_SUM))
        def _():
            total(t - LAG_SUM)

        @pl.when(t >= LAG_OUT)
        def _():
            finish(t - LAG_OUT)

        return carry

    lax.fori_loop(1, chunks + LAG_OUT, body, 0)

    def drain(i, carry):
        far_down(i).wait_send()
        far_up(i).wait_send()
        near_down(i).wait_send()
        near_up(i).wait_send()

        @pl.when(moves)
        def _():
            move(i).wait_send()

        o_store(i).wait()
        return carry

    lax.fori_loop(0, chunks, drain, 0)


def cannon_step(shift, p_matrix, s_matrix, p_pattern, s_pattern, c_input):
    rows, depth = p_matrix.shape
    chunks = rows // CHUNK
    width = c_input.shape[1]
    dma = pltpu.SemaphoreType.DMA
    half = lambda dtype, *lead: pltpu.VMEM((chunks, *lead, HALF, width), dtype)
    full = lambda dtype: pltpu.VMEM((chunks, CHUNK, width), dtype)
    return pl.pallas_call(
        functools.partial(kernel, shift, chunks),
        out_shape=jax.ShapeDtypeStruct(c_input.shape, jnp.float32),
        in_specs=[pl.BlockSpec(memory_space=pltpu.SMEM)] * 2 + [pl.BlockSpec(memory_space=pl.ANY)] * 3,
        out_specs=pl.BlockSpec(memory_space=pl.ANY),
        scratch_shapes=[
            pltpu.VMEM((chunks, CHUNK, depth), jnp.bfloat16),
            pltpu.VMEM((depth, 4 * width), jnp.bfloat16),
            pltpu.VMEM((rows, width), jnp.float32),
            full(jnp.float32),
            full(jnp.float32),
            half(jnp.float32), half(jnp.float32),
            half(jnp.bfloat16, 2),
            full(jnp.bfloat16), full(jnp.bfloat16), full(jnp.bfloat16),
            half(jnp.bfloat16, 2),
            full(jnp.bfloat16), full(jnp.bfloat16), full(jnp.bfloat16),
            dma((chunks,)), dma((4,)), dma, dma((chunks,)),
            dma((chunks, 2)), dma((chunks, 2)),
            dma((chunks,)), dma((chunks,)), dma((chunks,)), dma((chunks,)),
            dma((chunks,)), dma((chunks,)),
        ],
        compiler_params=pltpu.CompilerParams(
            collective_id=shift, has_side_effects=True, vmem_limit_bytes=56 * 2**20
        ),
        cost_estimate=pl.CostEstimate(
            flops=2 * rows * depth * 4 * width, bytes_accessed=20 * 2**20, transcendentals=0
        ),
    )(p_pattern, s_pattern, p_matrix, s_matrix, c_input)


def local(p_matrix, s_matrix, p_pattern, s_pattern, c_input, step):
    return lax.switch(
        lax.rem(step[0], 4),
        [functools.partial(cannon_step, shift) for shift in range(4)],
        p_matrix, s_matrix, p_pattern, s_pattern, c_input,
    )


def solution(mesh):
    placed = (
        P("row", ("col", "rep")),
        P(("col", "rep"), None),
        P("row", ("col", "rep")),
        P(("col", "rep"), None),
        P("row", ("col", "rep")),
        P(),
    )
    return jax.shard_map(
        local, mesh=mesh, in_specs=placed, out_specs=P("row", ("col", "rep")), check_vma=False
    )
```

```python
import functools

import jax
import jax.numpy as jnp
from jax import lax
from jax.experimental import pallas as pl
from jax.experimental.pallas import tpu as pltpu
from jax.sharding import PartitionSpec as P

BLOCK = 128
CHUNK = 512
HALF = CHUNK // 2
EARLY = 2
AHEAD = 2
LAG_ADD, LAG_SUM, LAG_OUT = 2, 4, 6
MESH = pl.DeviceIdType.MESH


def kernel(
    shift, chunks, pp_hbm, sp_hbm, p_hbm, s_hbm, c_hbm, o_hbm,
    p_pat, s_pat, p_v, s_v, c_v, o_v, own, wait_lo, wait_hi, far_s, lo_s, hi_s, move_s, mid_s,
    far_r, lo_r, hi_r, move_r, mid_r,
    pat_sem, p_sem, s_sem, c_sem, o_sem, far_ss, far_rs, lo_ss, lo_rs, hi_ss, hi_rs,
    move_ss, move_rs, mid_ss, mid_rs,
):
    row, col, rep = lax.axis_index("row"), lax.axis_index("col"), lax.axis_index("rep")
    distance = lax.rem(row + shift, 4)
    target = lax.rem(col + 4 - distance, 4)
    origin = lax.rem(col + distance, 4)
    group = target
    up, down, across = {"rep": lax.rem(rep + 1, 4)}, {"rep": lax.rem(rep + 3, 4)}, {"col": target}
    moves = distance != 0
    stays = distance == 0

    barrier = pltpu.get_barrier_semaphore()
    for neighbour in (up, down):
        pl.semaphore_signal(barrier, inc=1, device_id=neighbour, device_id_type=MESH)

    @pl.when(moves)
    def _():
        pl.semaphore_signal(barrier, inc=1, device_id=across, device_id_type=MESH)
        pl.semaphore_signal(barrier, inc=1, device_id={"col": origin}, device_id_type=MESH)

    def s_load(k):
        at = pl.multiple_of((group * 4 + lax.rem(rep + k, 4)) * BLOCK, BLOCK)
        return pltpu.make_async_copy(
            s_hbm.at[:, pl.ds(at, BLOCK)], s_v.at[:, pl.ds(k * BLOCK, BLOCK)], s_sem.at[k]
        )

    def p_load(i):
        return pltpu.make_async_copy(p_hbm.at[pl.ds(i * CHUNK, CHUNK)], p_v.at[i], p_sem.at[i])

    def c_load(i):
        at = pl.ds(i * CHUNK, CHUNK)
        return pltpu.make_async_copy(c_hbm.at[at], c_v.at[i], c_sem.at[i])

    def o_store(i):
        return pltpu.make_async_copy(o_v.at[i], o_hbm.at[pl.ds(i * CHUNK, CHUNK)], o_sem)

    def remote(source, target_ref, send, receive, device):
        return pltpu.make_async_remote_copy(
            src_ref=source, dst_ref=target_ref, send_sem=send, recv_sem=receive,
            device_id=device, device_id_type=MESH,
        )

    def far_down(i):
        return remote(far_s.at[i, 0], far_r.at[i, 0], far_ss, far_rs.at[i, 0], down)

    def far_up(i):
        return remote(far_s.at[i, 1], far_r.at[i, 1], far_ss, far_rs.at[i, 1], up)

    def near_down(i, source=None):
        source = lo_s.at[i] if source is None else source
        return remote(source, hi_r.at[i], lo_ss, hi_rs.at[i], down)

    def near_up(i, source=None):
        source = hi_s.at[i] if source is None else source
        return remote(source, lo_r.at[i], hi_ss, lo_rs.at[i], up)

    def move(i):
        at = i - EARLY
        return remote(move_s.at[at], move_r.at[at], move_ss, move_rs.at[at], across)

    def middle(i):
        return remote(mid_s.at[i], mid_r.at[i], mid_ss, mid_rs.at[i], across)

    pat_copies = [
        pltpu.make_async_copy(pp_hbm, p_pat, pat_sem.at[0]),
        pltpu.make_async_copy(sp_hbm, s_pat, pat_sem.at[1]),
    ]
    pat_copies[1].start()
    pat_copies[0].start()
    for k in range(4):
        s_load(k).start()
    p_load(0).start()
    for i in range(1, AHEAD + 1):
        p_load(i).start()

    def as_scale(value):
        return value.astype(jnp.float32).astype(jnp.bfloat16)

    pat_copies[1].wait()
    for k in range(4):
        s_load(k).wait()
        for b in range(8):
            rows, columns = pl.ds(b * BLOCK, BLOCK), pl.ds(k * BLOCK, BLOCK)
            keep = as_scale(s_pat[b, group * 4 + lax.rem(rep + k, 4)])
            s_v[rows, columns] = s_v[rows, columns] * keep
    pat_copies[0].wait()

    def product(i):
        p_load(i).wait()
        for a in range(CHUNK // BLOCK):
            for b in range(8):
                rows, columns = pl.ds(a * BLOCK, BLOCK), pl.ds(b * BLOCK, BLOCK)
                keep = as_scale(p_pat[b, i * (CHUNK // BLOCK) + a])
                p_v[i, rows, columns] = p_v[i, rows, columns] * keep
        return jnp.dot(p_v[i], s_v[...], preferred_element_type=jnp.float32)

    def share(i, term):
        far = term[:, 2 * BLOCK:3 * BLOCK].astype(jnp.bfloat16)
        far_s[i, 0] = far[:HALF]
        far_s[i, 1] = far[HALF:]
        far_down(i).start()
        far_up(i).start()
        own[i] = term[:, :BLOCK].astype(jnp.float32)
        hi_s[i, :HALF] = term[:HALF, BLOCK:2 * BLOCK].astype(jnp.bfloat16)
        wait_hi[i] = term[HALF:, BLOCK:2 * BLOCK].astype(jnp.float32)
        wait_lo[i] = term[:HALF, 3 * BLOCK:].astype(jnp.float32)
        lo_s[i, HALF:] = term[HALF:, 3 * BLOCK:].astype(jnp.bfloat16)

    def add(i):
        c_load(i).start()
        far_down(i).wait_recv()
        lo_s[i, :HALF] = (wait_lo[i] + far_r[i, 0].astype(jnp.float32)).astype(jnp.bfloat16)

        @pl.when(i >= EARLY)
        def _():
            near_down(i).start()

        far_up(i).wait_recv()
        hi_s[i, HALF:] = (wait_hi[i] + far_r[i, 1].astype(jnp.float32)).astype(jnp.bfloat16)

        @pl.when(i >= EARLY)
        def _():
            near_up(i).start()

        def gather(to):
            to[i, 0] = lo_s[i]
            to[i, 1] = hi_s[i]
            to[i, 2] = own[i].astype(jnp.bfloat16)

        @pl.when(jnp.logical_and(i < EARLY, moves))
        def _():
            gather(mid_s)
            middle(i).start()

        @pl.when(jnp.logical_and(i < EARLY, stays))
        def _():
            gather(mid_r)

    def resume(i):
        @pl.when(moves)
        def _():
            middle(i).wait_recv()

        near_down(i, mid_r.at[i, 0]).start()
        near_up(i, mid_r.at[i, 1]).start()

    def put(i, value):
        c_load(i).wait()
        o_v[i] = c_v[i] + value
        o_store(i).start()

    def arrived(i):
        near_down(i).wait_recv()
        near_up(i).wait_recv()
        return hi_r[i].astype(jnp.float32) + lo_r[i].astype(jnp.float32)

    def total(i):
        summed = own[i] + arrived(i)

        @pl.when(moves)
        def _():
            move_s[i - EARLY] = summed.astype(jnp.bfloat16)
            move(i).start()

        @pl.when(stays)
        def _():
            put(i, summed)

    def total_early(i):
        put(i, mid_r[i, 2].astype(jnp.float32) + arrived(i))

    def finish(i):
        move(i).wait_recv()
        put(i, move_r[i - EARLY].astype(jnp.float32))

    initial = product(0)

    @pl.when(moves)
    def _():
        pl.semaphore_wait(barrier, 4)

    @pl.when(stays)
    def _():
        pl.semaphore_wait(barrier, 2)

    share(0, initial)

    def within(value, low, high):
        return jnp.logical_and(value >= low, value < high)

    def body(t, carry):
        @pl.when(t + AHEAD < chunks)
        def _():
            p_load(t + AHEAD).start()

        @pl.when(t < chunks)
        def _():
            share(t, product(t))

        @pl.when(within(t, LAG_ADD, chunks + LAG_ADD))
        def _():
            add(t - LAG_ADD)

        @pl.when(within(t, chunks + LAG_ADD, chunks + EARLY + LAG_ADD))
        def _():
            resume(t - chunks - LAG_ADD)

        @pl.when(within(t, EARLY + LAG_SUM, chunks + LAG_SUM))
        def _():
            total(t - LAG_SUM)

        @pl.when(within(t, chunks + LAG_SUM, chunks + EARLY + LAG_SUM))
        def _():
            total_early(t - chunks - LAG_SUM)

        @pl.when(jnp.logical_and(moves, within(t, EARLY + LAG_OUT, chunks + LAG_OUT)))
        def _():
            finish(t - LAG_OUT)

        return carry

    lax.fori_loop(1, max(chunks + EARLY + LAG_SUM, chunks + LAG_OUT), body, 0)

    remote(far_s, far_r, far_ss, far_rs.at[0, 0], down).wait_send()
    remote(lo_s, hi_r, lo_ss, hi_rs.at[0], down).wait_send()
    remote(hi_s, lo_r, hi_ss, lo_rs.at[0], up).wait_send()

    @pl.when(moves)
    def _():
        remote(move_s, move_r, move_ss, move_rs.at[0], across).wait_send()
        remote(mid_s, mid_r, mid_ss, mid_rs.at[0], across).wait_send()

    pltpu.make_async_copy(o_hbm, o_hbm, o_sem).wait()


def cannon_step(shift, p_matrix, s_matrix, p_pattern, s_pattern, c_input):
    rows, depth = p_matrix.shape
    chunks = rows // CHUNK
    width = c_input.shape[1]
    plain = chunks - EARLY
    dma = pltpu.SemaphoreType.DMA
    half = lambda dtype, *lead: pltpu.VMEM((chunks, *lead, HALF, width), dtype)
    full = lambda dtype, count=chunks: pltpu.VMEM((count, CHUNK, width), dtype)
    early = pltpu.VMEM((EARLY, 3, CHUNK, width), jnp.bfloat16)
    return pl.pallas_call(
        functools.partial(kernel, shift, chunks),
        out_shape=jax.ShapeDtypeStruct(c_input.shape, jnp.float32),
        in_specs=[pl.BlockSpec(memory_space=pl.ANY)] * 5,
        out_specs=pl.BlockSpec(memory_space=pl.ANY),
        scratch_shapes=[
            pltpu.SMEM(p_pattern.shape, jnp.int32), pltpu.SMEM(s_pattern.shape, jnp.int32),
            pltpu.VMEM((chunks, CHUNK, depth), jnp.bfloat16),
            pltpu.VMEM((depth, 4 * width), jnp.bfloat16),
            full(jnp.float32), full(jnp.float32), full(jnp.float32),
            half(jnp.float32), half(jnp.float32),
            half(jnp.bfloat16, 2),
            full(jnp.bfloat16), full(jnp.bfloat16), full(jnp.bfloat16, plain), early,
            half(jnp.bfloat16, 2),
            full(jnp.bfloat16), full(jnp.bfloat16), full(jnp.bfloat16, plain), early,
            dma((2,)), dma((chunks,)), dma((4,)), dma((chunks,)), dma,
            dma, dma((chunks, 2)),
            dma, dma((chunks,)), dma, dma((chunks,)),
            dma, dma((plain,)), dma, dma((EARLY,)),
        ],
        compiler_params=pltpu.CompilerParams(
            collective_id=shift, has_side_effects=True, vmem_limit_bytes=56 * 2**20
        ),
        cost_estimate=pl.CostEstimate(
            flops=2 * rows * depth * 4 * width, bytes_accessed=20 * 2**20, transcendentals=0
        ),
    )(p_pattern, s_pattern, p_matrix, s_matrix, c_input)


def local(p_matrix, s_matrix, p_pattern, s_pattern, c_input, step):
    return lax.switch(
        lax.rem(step[0], 4),
        [functools.partial(cannon_step, shift) for shift in range(4)],
        p_matrix, s_matrix, p_pattern.T, s_pattern, c_input,
    )


def solution(mesh):
    placed = (
        P("row", ("col", "rep")),
        P(("col", "rep"), None),
        P("row", ("col", "rep")),
        P(("col", "rep"), None),
        P("row", ("col", "rep")),
        P(),
    )
    return jax.shard_map(
        local, mesh=mesh, in_specs=placed, out_specs=P("row", ("col", "rep")), check_vma=False
    )
```

```python
import functools

import jax
import jax.numpy as jnp
from jax import lax
from jax.experimental import pallas as pl
from jax.experimental.pallas import tpu as pltpu
from jax.sharding import PartitionSpec as P

BLOCK = 128
CHUNK = 512
HALF = CHUNK // 2
EARLY = 2
AHEAD = 1
LAG_ADD, LAG_SUM, LAG_OUT = 3, 5, 7
MESH = pl.DeviceIdType.MESH


def kernel(
    shift, chunks, pp_hbm, sp_hbm, p_hbm, s_hbm, c_hbm, o_hbm,
    p_pat, s_pat, p_v, s_v, c_v, o_v, own, wait_lo, wait_hi, far_s, lo_s, hi_s, move_s, mid_s,
    far_r, lo_r, hi_r, move_r, mid_r,
    pat_sem, p_sem, s_sem, c_sem, o_sem, far_ss, far_rs, lo_ss, lo_rs, hi_ss, hi_rs,
    move_ss, move_rs, mid_ss, mid_rs,
):
    row, col, rep = lax.axis_index("row"), lax.axis_index("col"), lax.axis_index("rep")
    distance = lax.rem(row + shift, 4)
    target = lax.rem(col + 4 - distance, 4)
    origin = lax.rem(col + distance, 4)
    group = target
    up, down, across = {"rep": lax.rem(rep + 1, 4)}, {"rep": lax.rem(rep + 3, 4)}, {"col": target}
    moves = distance != 0
    stays = distance == 0

    barrier = pltpu.get_barrier_semaphore()
    for neighbour in (up, down):
        pl.semaphore_signal(barrier, inc=1, device_id=neighbour, device_id_type=MESH)

    @pl.when(moves)
    def _():
        pl.semaphore_signal(barrier, inc=1, device_id=across, device_id_type=MESH)
        pl.semaphore_signal(barrier, inc=1, device_id={"col": origin}, device_id_type=MESH)

    def s_load(k):
        at = pl.multiple_of((group * 4 + lax.rem(rep + k, 4)) * BLOCK, BLOCK)
        return pltpu.make_async_copy(
            s_hbm.at[:, pl.ds(at, BLOCK)], s_v.at[:, pl.ds(k * BLOCK, BLOCK)], s_sem.at[k]
        )

    def p_load(i):
        return pltpu.make_async_copy(p_hbm.at[pl.ds(i * CHUNK, CHUNK)], p_v.at[i], p_sem.at[i])

    def c_load(i):
        at = pl.ds(i * CHUNK, CHUNK)
        return pltpu.make_async_copy(c_hbm.at[at], c_v.at[i], c_sem.at[i])

    def o_store(i):
        return pltpu.make_async_copy(o_v.at[i], o_hbm.at[pl.ds(i * CHUNK, CHUNK)], o_sem)

    def remote(source, target_ref, send, receive, device):
        return pltpu.make_async_remote_copy(
            src_ref=source, dst_ref=target_ref, send_sem=send, recv_sem=receive,
            device_id=device, device_id_type=MESH,
        )

    def far_down(i):
        return remote(far_s.at[i, 0], far_r.at[i, 0], far_ss, far_rs.at[i, 0], down)

    def far_up(i):
        return remote(far_s.at[i, 1], far_r.at[i, 1], far_ss, far_rs.at[i, 1], up)

    def near_down(i, source=None):
        source = lo_s.at[i] if source is None else source
        return remote(source, hi_r.at[i], lo_ss, hi_rs.at[i], down)

    def near_up(i, source=None):
        source = hi_s.at[i] if source is None else source
        return remote(source, lo_r.at[i], hi_ss, lo_rs.at[i], up)

    def move(i):
        at = i - EARLY
        return remote(move_s.at[at], move_r.at[at], move_ss, move_rs.at[at], across)

    def middle(i):
        return remote(mid_s.at[i], mid_r.at[i], mid_ss, mid_rs.at[i], across)

    pat_copies = [
        pltpu.make_async_copy(pp_hbm, p_pat, pat_sem.at[0]),
        pltpu.make_async_copy(sp_hbm, s_pat, pat_sem.at[1]),
    ]
    pat_copies[1].start()
    pat_copies[0].start()
    for k in range(4):
        s_load(k).start()
    p_load(0).start()
    for i in range(1, AHEAD + 1):
        p_load(i).start()

    def as_scale(value):
        return value.astype(jnp.float32).astype(jnp.bfloat16)

    pat_copies[1].wait()
    for k in range(4):
        s_load(k).wait()
        for b in range(8):
            rows, columns = pl.ds(b * BLOCK, BLOCK), pl.ds(k * BLOCK, BLOCK)
            keep = as_scale(s_pat[b, group * 4 + lax.rem(rep + k, 4)])
            s_v[rows, columns] = s_v[rows, columns] * keep
    pat_copies[0].wait()

    def product(i):
        p_load(i).wait()
        for a in range(CHUNK // BLOCK):
            for b in range(8):
                rows, columns = pl.ds(a * BLOCK, BLOCK), pl.ds(b * BLOCK, BLOCK)
                keep = as_scale(p_pat[b, i * (CHUNK // BLOCK) + a])
                p_v[i, rows, columns] = p_v[i, rows, columns] * keep
        return jnp.dot(p_v[i], s_v[...], preferred_element_type=jnp.float32)

    def share(i, term):
        far = term[:, 2 * BLOCK:3 * BLOCK].astype(jnp.bfloat16)
        far_s[i, 0] = far[:HALF]
        far_s[i, 1] = far[HALF:]
        far_down(i).start()
        far_up(i).start()
        own[i] = term[:, :BLOCK].astype(jnp.float32)
        hi_s[i, :HALF] = term[:HALF, BLOCK:2 * BLOCK].astype(jnp.bfloat16)
        wait_hi[i] = term[HALF:, BLOCK:2 * BLOCK].astype(jnp.float32)
        wait_lo[i] = term[:HALF, 3 * BLOCK:].astype(jnp.float32)
        lo_s[i, HALF:] = term[HALF:, 3 * BLOCK:].astype(jnp.bfloat16)

    def add(i):
        c_load(i).start()
        far_down(i).wait_recv()
        lo_s[i, :HALF] = (wait_lo[i] + far_r[i, 0].astype(jnp.float32)).astype(jnp.bfloat16)

        @pl.when(i >= EARLY)
        def _():
            near_down(i).start()

        far_up(i).wait_recv()
        hi_s[i, HALF:] = (wait_hi[i] + far_r[i, 1].astype(jnp.float32)).astype(jnp.bfloat16)

        @pl.when(i >= EARLY)
        def _():
            near_up(i).start()

        def gather(to):
            to[i, 0] = lo_s[i]
            to[i, 1] = hi_s[i]
            to[i, 2] = own[i].astype(jnp.bfloat16)

        @pl.when(jnp.logical_and(i < EARLY, moves))
        def _():
            gather(mid_s)
            middle(i).start()

        @pl.when(jnp.logical_and(i < EARLY, stays))
        def _():
            gather(mid_r)

    def resume(i):
        @pl.when(moves)
        def _():
            middle(i).wait_recv()

        near_down(i, mid_r.at[i, 0]).start()
        near_up(i, mid_r.at[i, 1]).start()

    def put(i, value):
        c_load(i).wait()
        o_v[i] = c_v[i] + value
        o_store(i).start()

    def arrived(i):
        near_down(i).wait_recv()
        near_up(i).wait_recv()
        return hi_r[i].astype(jnp.float32) + lo_r[i].astype(jnp.float32)

    def total(i):
        summed = own[i] + arrived(i)

        @pl.when(moves)
        def _():
            move_s[i - EARLY] = summed.astype(jnp.bfloat16)
            move(i).start()

        @pl.when(stays)
        def _():
            put(i, summed)

    def total_early(i):
        put(i, mid_r[i, 2].astype(jnp.float32) + arrived(i))

    def finish(i):
        move(i).wait_recv()
        put(i, move_r[i - EARLY].astype(jnp.float32))

    initial = product(0)

    @pl.when(moves)
    def _():
        pl.semaphore_wait(barrier, 4)

    @pl.when(stays)
    def _():
        pl.semaphore_wait(barrier, 2)

    share(0, initial)

    def within(value, low, high):
        return jnp.logical_and(value >= low, value < high)

    def body(t, carry):
        @pl.when(t + AHEAD < chunks)
        def _():
            p_load(t + AHEAD).start()

        @pl.when(t < chunks)
        def _():
            share(t, product(t))

        @pl.when(within(t, LAG_ADD, chunks + LAG_ADD))
        def _():
            add(t - LAG_ADD)

        @pl.when(within(t, chunks + LAG_ADD, chunks + EARLY + LAG_ADD))
        def _():
            resume(t - chunks - LAG_ADD)

        @pl.when(within(t, EARLY + LAG_SUM, chunks + LAG_SUM))
        def _():
            total(t - LAG_SUM)

        @pl.when(within(t, chunks + LAG_SUM, chunks + EARLY + LAG_SUM))
        def _():
            total_early(t - chunks - LAG_SUM)

        @pl.when(jnp.logical_and(moves, within(t, EARLY + LAG_OUT, chunks + LAG_OUT)))
        def _():
            finish(t - LAG_OUT)

        return carry

    lax.fori_loop(1, max(chunks + EARLY + LAG_SUM, chunks + LAG_OUT), body, 0)

    remote(far_s, far_r, far_ss, far_rs.at[0, 0], down).wait_send()
    remote(lo_s, hi_r, lo_ss, hi_rs.at[0], down).wait_send()
    remote(hi_s, lo_r, hi_ss, lo_rs.at[0], up).wait_send()

    @pl.when(moves)
    def _():
        remote(move_s, move_r, move_ss, move_rs.at[0], across).wait_send()
        remote(mid_s, mid_r, mid_ss, mid_rs.at[0], across).wait_send()

    pltpu.make_async_copy(o_hbm, o_hbm, o_sem).wait()


def cannon_step(shift, p_matrix, s_matrix, p_pattern, s_pattern, c_input):
    rows, depth = p_matrix.shape
    chunks = rows // CHUNK
    width = c_input.shape[1]
    plain = chunks - EARLY
    dma = pltpu.SemaphoreType.DMA
    half = lambda dtype, *lead: pltpu.VMEM((chunks, *lead, HALF, width), dtype)
    full = lambda dtype, count=chunks: pltpu.VMEM((count, CHUNK, width), dtype)
    early = pltpu.VMEM((EARLY, 3, CHUNK, width), jnp.bfloat16)
    return pl.pallas_call(
        functools.partial(kernel, shift, chunks),
        out_shape=jax.ShapeDtypeStruct(c_input.shape, jnp.float32),
        in_specs=[pl.BlockSpec(memory_space=pl.ANY)] * 5,
        out_specs=pl.BlockSpec(memory_space=pl.ANY),
        scratch_shapes=[
            pltpu.SMEM(p_pattern.shape, jnp.int32), pltpu.SMEM(s_pattern.shape, jnp.int32),
            pltpu.VMEM((chunks, CHUNK, depth), jnp.bfloat16),
            pltpu.VMEM((depth, 4 * width), jnp.bfloat16),
            full(jnp.float32), full(jnp.float32), full(jnp.float32),
            half(jnp.float32), half(jnp.float32),
            half(jnp.bfloat16, 2),
            full(jnp.bfloat16), full(jnp.bfloat16), full(jnp.bfloat16, plain), early,
            half(jnp.bfloat16, 2),
            full(jnp.bfloat16), full(jnp.bfloat16), full(jnp.bfloat16, plain), early,
            dma((2,)), dma((chunks,)), dma((4,)), dma((chunks,)), dma,
            dma, dma((chunks, 2)),
            dma, dma((chunks,)), dma, dma((chunks,)),
            dma, dma((plain,)), dma, dma((EARLY,)),
        ],
        compiler_params=pltpu.CompilerParams(
            collective_id=shift, has_side_effects=True, vmem_limit_bytes=56 * 2**20
        ),
        cost_estimate=pl.CostEstimate(
            flops=2 * rows * depth * 4 * width, bytes_accessed=20 * 2**20, transcendentals=0
        ),
    )(p_pattern, s_pattern, p_matrix, s_matrix, c_input)


def local(p_matrix, s_matrix, p_pattern, s_pattern, c_input, step):
    return lax.switch(
        step[0] & 3,
        [functools.partial(cannon_step, shift) for shift in range(4)],
        p_matrix, s_matrix, p_pattern.T, s_pattern, c_input,
    )


def solution(mesh):
    placed = (
        P("row", ("col", "rep")),
        P(("col", "rep"), None),
        P("row", ("col", "rep")),
        P(("col", "rep"), None),
        P("row", ("col", "rep")),
        P(),
    )
    return jax.shard_map(
        local, mesh=mesh, in_specs=placed, out_specs=P("row", ("col", "rep")), check_vma=False
    )
```

```python
import functools

import jax
import jax.numpy as jnp
from jax import lax
from jax.experimental import pallas as pl
from jax.experimental.pallas import tpu as pltpu
from jax.sharding import PartitionSpec as P

BLOCK = 128
CHUNK = 512
HALF = CHUNK // 2
EARLY = 2
AHEAD = 1
SLOTS = (0, 1, 3, 2)
HEAD = 2
LAG_ADD, LAG_SUM, LAG_OUT = 3, 5, 7
MESH = pl.DeviceIdType.MESH


def kernel(
    shift, chunks, pp_hbm, sp_hbm, p_hbm, s_hbm, c_hbm, o_hbm,
    p_pat, s_pat, p_v, s_v, c_v, o_v, own, wait_lo, wait_hi, far_s, lo_s, hi_s, move_s, mid_s,
    far_r, lo_r, hi_r, move_r, mid_r,
    pat_sem, p_sem, s_sem, c_sem, o_sem, far_ss, far_rs, lo_ss, lo_rs, hi_ss, hi_rs,
    move_ss, move_rs, mid_ss, mid_rs,
):
    row, col, rep = lax.axis_index("row"), lax.axis_index("col"), lax.axis_index("rep")
    distance = lax.rem(row + shift, 4)
    target = lax.rem(col + 4 - distance, 4)
    origin = lax.rem(col + distance, 4)
    group = target
    up, down, across = {"rep": lax.rem(rep + 1, 4)}, {"rep": lax.rem(rep + 3, 4)}, {"col": target}
    moves = distance != 0
    stays = distance == 0

    barrier = pltpu.get_barrier_semaphore()
    for neighbour in (up, down):
        pl.semaphore_signal(barrier, inc=1, device_id=neighbour, device_id_type=MESH)

    @pl.when(moves)
    def _():
        pl.semaphore_signal(barrier, inc=1, device_id=across, device_id_type=MESH)
        pl.semaphore_signal(barrier, inc=1, device_id={"col": origin}, device_id_type=MESH)

    def s_block(k):
        return group * 4 + lax.rem(rep + SLOTS[k], 4)

    def s_load(k):
        at = pl.multiple_of(s_block(k) * BLOCK, BLOCK)
        return pltpu.make_async_copy(
            s_hbm.at[:, pl.ds(at, BLOCK)], s_v.at[:, pl.ds(k * BLOCK, BLOCK)], s_sem.at[k]
        )

    def p_load(i):
        return pltpu.make_async_copy(p_hbm.at[pl.ds(i * CHUNK, CHUNK)], p_v.at[i], p_sem.at[i])

    def p_first(half):
        at = pl.ds(half * HALF, HALF)
        return pltpu.make_async_copy(p_hbm.at[at], p_v.at[0, at], p_sem.at[half * chunks])

    def c_load(i):
        at = pl.ds(i * CHUNK, CHUNK)
        return pltpu.make_async_copy(c_hbm.at[at], c_v.at[i], c_sem.at[i])

    def o_store(i):
        return pltpu.make_async_copy(o_v.at[i], o_hbm.at[pl.ds(i * CHUNK, CHUNK)], o_sem)

    def remote(source, target_ref, send, receive, device):
        return pltpu.make_async_remote_copy(
            src_ref=source, dst_ref=target_ref, send_sem=send, recv_sem=receive,
            device_id=device, device_id_type=MESH,
        )

    def far_down(i):
        return remote(far_s.at[i, 0], far_r.at[i, 0], far_ss, far_rs.at[i, 0], down)

    def far_up(i):
        return remote(far_s.at[i, 1], far_r.at[i, 1], far_ss, far_rs.at[i, 1], up)

    def near_down(i, source=None):
        source = lo_s.at[i] if source is None else source
        return remote(source, hi_r.at[i], lo_ss, hi_rs.at[i], down)

    def near_up(i, source=None):
        source = hi_s.at[i] if source is None else source
        return remote(source, lo_r.at[i], hi_ss, lo_rs.at[i], up)

    def move(i):
        at = i - EARLY
        return remote(move_s.at[at], move_r.at[at], move_ss, move_rs.at[at], across)

    def middle(i):
        return remote(mid_s.at[i], mid_r.at[i], mid_ss, mid_rs.at[i], across)

    pat_copies = [
        pltpu.make_async_copy(pp_hbm, p_pat, pat_sem.at[0]),
        pltpu.make_async_copy(sp_hbm, s_pat, pat_sem.at[1]),
    ]
    pat_copies[1].start()
    pat_copies[0].start()
    s_load(3).start()
    p_first(0).start()
    p_first(1).start()
    p_load(1).start()
    for k in range(3):
        s_load(k).start()
    for i in range(2, HEAD + AHEAD):
        p_load(i).start()

    def as_scale(value):
        return value.astype(jnp.float32).astype(jnp.bfloat16)

    def mask_s(k):
        s_load(k).wait()
        for b in range(8):
            rows, columns = pl.ds(b * BLOCK, BLOCK), pl.ds(k * BLOCK, BLOCK)
            s_v[rows, columns] = s_v[rows, columns] * as_scale(s_pat[b, s_block(k)])

    def mask_p(i, low, high):
        for a in range(low, high):
            for b in range(8):
                rows, columns = pl.ds(a * BLOCK, BLOCK), pl.ds(b * BLOCK, BLOCK)
                keep = as_scale(p_pat[b, i * (CHUNK // BLOCK) + a])
                p_v[i, rows, columns] = p_v[i, rows, columns] * keep

    def send_far(i):
        far_down(i).start()
        far_up(i).start()

    def far_part(i, half):
        left = p_v[i, pl.ds(half * HALF, HALF)]
        far = jnp.dot(left, s_v[:, 3 * BLOCK:], preferred_element_type=jnp.float32)
        far_s[i, half] = far.astype(jnp.bfloat16)

    def keep_near(i, term):
        own[i] = term[:, :BLOCK]
        hi_s[i, :HALF] = term[:HALF, BLOCK:2 * BLOCK].astype(jnp.bfloat16)
        wait_hi[i] = term[HALF:, BLOCK:2 * BLOCK]
        wait_lo[i] = term[:HALF, 2 * BLOCK:3 * BLOCK]
        lo_s[i, HALF:] = term[HALF:, 2 * BLOCK:3 * BLOCK].astype(jnp.bfloat16)

    def produce(i):
        p_load(i).wait()
        mask_p(i, 0, CHUNK // BLOCK)
        term = jnp.dot(p_v[i], s_v[...], preferred_element_type=jnp.float32)
        far = term[:, 3 * BLOCK:].astype(jnp.bfloat16)
        far_s[i, 0] = far[:HALF]
        far_s[i, 1] = far[HALF:]
        send_far(i)
        keep_near(i, term)

    def add(i):
        c_load(i).start()
        far_down(i).wait_recv()
        lo_s[i, :HALF] = (wait_lo[i] + far_r[i, 0].astype(jnp.float32)).astype(jnp.bfloat16)

        @pl.when(i >= EARLY)
        def _():
            near_down(i).start()

        far_up(i).wait_recv()
        hi_s[i, HALF:] = (wait_hi[i] + far_r[i, 1].astype(jnp.float32)).astype(jnp.bfloat16)

        @pl.when(i >= EARLY)
        def _():
            near_up(i).start()

        def gather(to):
            to[i, 0] = lo_s[i]
            to[i, 1] = hi_s[i]
            to[i, 2] = own[i].astype(jnp.bfloat16)

        @pl.when(jnp.logical_and(i < EARLY, moves))
        def _():
            gather(mid_s)
            middle(i).start()

        @pl.when(jnp.logical_and(i < EARLY, stays))
        def _():
            gather(mid_r)

    def resume(i):
        @pl.when(moves)
        def _():
            middle(i).wait_recv()

        near_down(i, mid_r.at[i, 0]).start()
        near_up(i, mid_r.at[i, 1]).start()

    def put(i, value):
        c_load(i).wait()
        o_v[i] = c_v[i] + value
        o_store(i).start()

    def arrived(i):
        near_down(i).wait_recv()
        near_up(i).wait_recv()
        return hi_r[i].astype(jnp.float32) + lo_r[i].astype(jnp.float32)

    def total(i):
        summed = own[i] + arrived(i)

        @pl.when(moves)
        def _():
            move_s[i - EARLY] = summed.astype(jnp.bfloat16)
            move(i).start()

        @pl.when(stays)
        def _():
            put(i, summed)

    def total_early(i):
        put(i, mid_r[i, 2].astype(jnp.float32) + arrived(i))

    def finish(i):
        move(i).wait_recv()
        put(i, move_r[i - EARLY].astype(jnp.float32))

    pat_copies[1].wait()
    mask_s(3)
    pat_copies[0].wait()
    for half in range(2):
        p_first(half).wait()
        mask_p(0, half * HALF // BLOCK, (half + 1) * HALF // BLOCK)
        far_part(0, half)

    @pl.when(moves)
    def _():
        pl.semaphore_wait(barrier, 4)

    @pl.when(stays)
    def _():
        pl.semaphore_wait(barrier, 2)

    send_far(0)
    for i in range(1, HEAD):
        p_load(i).wait()
        mask_p(i, 0, CHUNK // BLOCK)
        far_part(i, 0)
        far_part(i, 1)
        send_far(i)
    for k in range(3):
        mask_s(k)
    for i in range(HEAD):
        keep_near(i, jnp.dot(p_v[i], s_v[:, :3 * BLOCK], preferred_element_type=jnp.float32))

    def within(value, low, high):
        return jnp.logical_and(value >= low, value < high)

    def body(t, carry):
        @pl.when(t + AHEAD < chunks)
        def _():
            p_load(t + AHEAD).start()

        @pl.when(t < chunks)
        def _():
            produce(t)

        @pl.when(within(t, LAG_ADD, chunks + LAG_ADD))
        def _():
            add(t - LAG_ADD)

        @pl.when(within(t, chunks + LAG_ADD, chunks + EARLY + LAG_ADD))
        def _():
            resume(t - chunks - LAG_ADD)

        @pl.when(within(t, EARLY + LAG_SUM, chunks + LAG_SUM))
        def _():
            total(t - LAG_SUM)

        @pl.when(within(t, chunks + LAG_SUM, chunks + EARLY + LAG_SUM))
        def _():
            total_early(t - chunks - LAG_SUM)

        @pl.when(jnp.logical_and(moves, within(t, EARLY + LAG_OUT, chunks + LAG_OUT)))
        def _():
            finish(t - LAG_OUT)

        return carry

    lax.fori_loop(HEAD, max(chunks + EARLY + LAG_SUM, chunks + LAG_OUT), body, 0)

    remote(far_s, far_r, far_ss, far_rs.at[0, 0], down).wait_send()
    remote(lo_s, hi_r, lo_ss, hi_rs.at[0], down).wait_send()
    remote(hi_s, lo_r, hi_ss, lo_rs.at[0], up).wait_send()

    @pl.when(moves)
    def _():
        remote(move_s, move_r, move_ss, move_rs.at[0], across).wait_send()
        remote(mid_s, mid_r, mid_ss, mid_rs.at[0], across).wait_send()

    pltpu.make_async_copy(o_hbm, o_hbm, o_sem).wait()


def cannon_step(shift, p_matrix, s_matrix, p_pattern, s_pattern, c_input):
    rows, depth = p_matrix.shape
    chunks = rows // CHUNK
    width = c_input.shape[1]
    plain = chunks - EARLY
    dma = pltpu.SemaphoreType.DMA
    half = lambda dtype, *lead: pltpu.VMEM((chunks, *lead, HALF, width), dtype)
    full = lambda dtype, count=chunks: pltpu.VMEM((count, CHUNK, width), dtype)
    early = pltpu.VMEM((EARLY, 3, CHUNK, width), jnp.bfloat16)
    return pl.pallas_call(
        functools.partial(kernel, shift, chunks),
        out_shape=jax.ShapeDtypeStruct(c_input.shape, jnp.float32),
        in_specs=[pl.BlockSpec(memory_space=pl.ANY)] * 5,
        out_specs=pl.BlockSpec(memory_space=pl.ANY),
        scratch_shapes=[
            pltpu.SMEM(p_pattern.shape, jnp.int32), pltpu.SMEM(s_pattern.shape, jnp.int32),
            pltpu.VMEM((chunks, CHUNK, depth), jnp.bfloat16),
            pltpu.VMEM((depth, 4 * width), jnp.bfloat16),
            full(jnp.float32), full(jnp.float32), full(jnp.float32),
            half(jnp.float32), half(jnp.float32),
            half(jnp.bfloat16, 2),
            full(jnp.bfloat16), full(jnp.bfloat16), full(jnp.bfloat16, plain), early,
            half(jnp.bfloat16, 2),
            full(jnp.bfloat16), full(jnp.bfloat16), full(jnp.bfloat16, plain), early,
            dma((2,)), dma((chunks + 1,)), dma((4,)), dma((chunks,)), dma,
            dma, dma((chunks, 2)),
            dma, dma((chunks,)), dma, dma((chunks,)),
            dma, dma((plain,)), dma, dma((EARLY,)),
        ],
        compiler_params=pltpu.CompilerParams(
            collective_id=shift, has_side_effects=True, vmem_limit_bytes=56 * 2**20
        ),
        cost_estimate=pl.CostEstimate(
            flops=2 * rows * depth * 4 * width, bytes_accessed=20 * 2**20, transcendentals=0
        ),
    )(p_pattern, s_pattern, p_matrix, s_matrix, c_input)


def local(p_matrix, s_matrix, p_pattern, s_pattern, c_input, step):
    return lax.switch(
        step[0] & 3,
        [functools.partial(cannon_step, shift) for shift in range(4)],
        p_matrix, s_matrix, p_pattern.T, s_pattern, c_input,
    )


def solution(mesh):
    placed = (
        P("row", ("col", "rep")),
        P(("col", "rep"), None),
        P("row", ("col", "rep")),
        P(("col", "rep"), None),
        P("row", ("col", "rep")),
        P(),
    )
    return jax.shard_map(
        local, mesh=mesh, in_specs=placed, out_specs=P("row", ("col", "rep")), check_vma=False
    )
```

```python
import functools

import jax
import jax.numpy as jnp
from jax import lax
from jax.experimental import pallas as pl
from jax.experimental.pallas import tpu as pltpu
from jax.sharding import PartitionSpec as P

BLOCK = 128
CHUNK = 512
HALF = CHUNK // 2
EARLY = 2
AHEAD = 1
LAG_ADD, LAG_SUM, LAG_OUT = 3, 5, 7
MESH = pl.DeviceIdType.MESH


def kernel(
    shift, chunks, pp_hbm, sp_hbm, p_hbm, s_hbm, c_hbm, o_hbm,
    p_pat, s_pat, p_v, s_v, c_v, o_v, own, wait_lo, wait_hi, far_s, lo_s, hi_s, move_s, mid_s,
    far_r, lo_r, hi_r, move_r, mid_r,
    pat_sem, p_sem, s_sem, c_sem, o_sem, far_ss, far_rs, lo_ss, lo_rs, hi_ss, hi_rs,
    move_ss, move_rs, mid_ss, mid_rs,
):
    row, col, rep = lax.axis_index("row"), lax.axis_index("col"), lax.axis_index("rep")
    distance = lax.rem(row + shift, 4)
    target = lax.rem(col + 4 - distance, 4)
    origin = lax.rem(col + distance, 4)
    group = target
    up, down, across = {"rep": lax.rem(rep + 1, 4)}, {"rep": lax.rem(rep + 3, 4)}, {"col": target}
    moves = distance != 0
    stays = distance == 0

    barrier = pltpu.get_barrier_semaphore()
    for neighbour in (up, down):
        pl.semaphore_signal(barrier, inc=1, device_id=neighbour, device_id_type=MESH)

    @pl.when(moves)
    def _():
        pl.semaphore_signal(barrier, inc=1, device_id=across, device_id_type=MESH)
        pl.semaphore_signal(barrier, inc=1, device_id={"col": origin}, device_id_type=MESH)

    def s_load(k):
        at = pl.multiple_of((group * 4 + lax.rem(rep + k, 4)) * BLOCK, BLOCK)
        return pltpu.make_async_copy(
            s_hbm.at[:, pl.ds(at, BLOCK)], s_v.at[:, pl.ds(k * BLOCK, BLOCK)], s_sem.at[k]
        )

    def p_load(i):
        return pltpu.make_async_copy(p_hbm.at[pl.ds(i * CHUNK, CHUNK)], p_v.at[i], p_sem.at[i])

    def c_load(i):
        at = pl.ds(i * CHUNK, CHUNK)
        return pltpu.make_async_copy(c_hbm.at[at], c_v.at[i], c_sem.at[i])

    def o_store(i):
        return pltpu.make_async_copy(o_v.at[i], o_hbm.at[pl.ds(i * CHUNK, CHUNK)], o_sem)

    def remote(source, target_ref, send, receive, device):
        return pltpu.make_async_remote_copy(
            src_ref=source, dst_ref=target_ref, send_sem=send, recv_sem=receive,
            device_id=device, device_id_type=MESH,
        )

    def far_down(i):
        return remote(far_s.at[i, 0], far_r.at[i, 0], far_ss, far_rs.at[i, 0], down)

    def far_up(i):
        return remote(far_s.at[i, 1], far_r.at[i, 1], far_ss, far_rs.at[i, 1], up)

    def near_down(i):
        return remote(lo_s.at[i], hi_r.at[i], lo_ss, hi_rs.at[i], down)

    def near_up(i):
        return remote(hi_s.at[i], lo_r.at[i], hi_ss, lo_rs.at[i], up)

    def end_down(i, half):
        at = pl.ds(half * HALF, HALF)
        return remote(mid_r.at[i, 0, at], hi_r.at[i, at], lo_ss, hi_rs.at[chunks + 2 * i + half], down)

    def end_up(i, half):
        at = pl.ds(half * HALF, HALF)
        return remote(mid_r.at[i, 1, at], lo_r.at[i, at], hi_ss, lo_rs.at[chunks + 2 * i + half], up)

    def move(i):
        at = i - EARLY
        return remote(move_s.at[at], move_r.at[at], move_ss, move_rs.at[at], across)

    def middle(i):
        return remote(mid_s.at[i], mid_r.at[i], mid_ss, mid_rs.at[i], across)

    pat_copies = [
        pltpu.make_async_copy(pp_hbm, p_pat, pat_sem.at[0]),
        pltpu.make_async_copy(sp_hbm, s_pat, pat_sem.at[1]),
    ]
    pat_copies[1].start()
    pat_copies[0].start()
    for k in range(4):
        s_load(k).start()
    p_load(0).start()
    for i in range(1, AHEAD + 1):
        p_load(i).start()

    def as_scale(value):
        return value.astype(jnp.float32).astype(jnp.bfloat16)

    pat_copies[1].wait()
    for k in range(4):
        s_load(k).wait()
        for b in range(8):
            rows, columns = pl.ds(b * BLOCK, BLOCK), pl.ds(k * BLOCK, BLOCK)
            keep = as_scale(s_pat[b, group * 4 + lax.rem(rep + k, 4)])
            s_v[rows, columns] = s_v[rows, columns] * keep
    pat_copies[0].wait()

    def product(i):
        p_load(i).wait()
        for a in range(CHUNK // BLOCK):
            for b in range(8):
                rows, columns = pl.ds(a * BLOCK, BLOCK), pl.ds(b * BLOCK, BLOCK)
                keep = as_scale(p_pat[b, i * (CHUNK // BLOCK) + a])
                p_v[i, rows, columns] = p_v[i, rows, columns] * keep
        return jnp.dot(p_v[i], s_v[...], preferred_element_type=jnp.float32)

    def share(i, term):
        far = term[:, 2 * BLOCK:3 * BLOCK].astype(jnp.bfloat16)
        far_s[i, 0] = far[:HALF]
        far_s[i, 1] = far[HALF:]
        far_down(i).start()
        far_up(i).start()
        own[i] = term[:, :BLOCK].astype(jnp.float32)
        hi_s[i, :HALF] = term[:HALF, BLOCK:2 * BLOCK].astype(jnp.bfloat16)
        wait_hi[i] = term[HALF:, BLOCK:2 * BLOCK].astype(jnp.float32)
        wait_lo[i] = term[:HALF, 3 * BLOCK:].astype(jnp.float32)
        lo_s[i, HALF:] = term[HALF:, 3 * BLOCK:].astype(jnp.bfloat16)

    def add(i):
        c_load(i).start()
        far_down(i).wait_recv()
        lo_s[i, :HALF] = (wait_lo[i] + far_r[i, 0].astype(jnp.float32)).astype(jnp.bfloat16)

        @pl.when(i >= EARLY)
        def _():
            near_down(i).start()

        far_up(i).wait_recv()
        hi_s[i, HALF:] = (wait_hi[i] + far_r[i, 1].astype(jnp.float32)).astype(jnp.bfloat16)

        @pl.when(i >= EARLY)
        def _():
            near_up(i).start()

        def gather(to):
            to[i, 0] = lo_s[i]
            to[i, 1] = hi_s[i]
            to[i, 2] = own[i].astype(jnp.bfloat16)

        @pl.when(jnp.logical_and(i < EARLY, moves))
        def _():
            gather(mid_s)
            middle(i).start()

        @pl.when(jnp.logical_and(i < EARLY, stays))
        def _():
            gather(mid_r)

    def resume(i):
        @pl.when(moves)
        def _():
            middle(i).wait_recv()

        for half in range(2):
            end_down(i, half).start()
            end_up(i, half).start()

    def put(i, value):
        c_load(i).wait()
        o_v[i] = c_v[i] + value
        o_store(i).start()

    def arrived(i):
        near_down(i).wait_recv()
        near_up(i).wait_recv()
        return hi_r[i].astype(jnp.float32) + lo_r[i].astype(jnp.float32)

    def total(i):
        summed = own[i] + arrived(i)

        @pl.when(moves)
        def _():
            move_s[i - EARLY] = summed.astype(jnp.bfloat16)
            move(i).start()

        @pl.when(stays)
        def _():
            put(i, summed)

    def total_early(i):
        c_load(i).wait()
        for half in range(2):
            at = pl.ds(half * HALF, HALF)
            end_down(i, half).wait_recv()
            end_up(i, half).wait_recv()
            both = hi_r[i, at].astype(jnp.float32) + lo_r[i, at].astype(jnp.float32)
            o_v[i, at] = c_v[i, at] + (mid_r[i, 2, at].astype(jnp.float32) + both)
            pltpu.make_async_copy(
                o_v.at[i, at], o_hbm.at[pl.ds(i * CHUNK + half * HALF, HALF)], o_sem
            ).start()

    def finish(i):
        move(i).wait_recv()
        put(i, move_r[i - EARLY].astype(jnp.float32))

    initial = product(0)

    @pl.when(moves)
    def _():
        pl.semaphore_wait(barrier, 4)

    @pl.when(stays)
    def _():
        pl.semaphore_wait(barrier, 2)

    share(0, initial)

    def within(value, low, high):
        return jnp.logical_and(value >= low, value < high)

    def body(t, carry):
        @pl.when(t + AHEAD < chunks)
        def _():
            p_load(t + AHEAD).start()

        @pl.when(t < chunks)
        def _():
            share(t, product(t))

        @pl.when(within(t, LAG_ADD, chunks + LAG_ADD))
        def _():
            add(t - LAG_ADD)

        @pl.when(within(t, chunks + LAG_ADD, chunks + EARLY + LAG_ADD))
        def _():
            resume(t - chunks - LAG_ADD)

        @pl.when(within(t, EARLY + LAG_SUM, chunks + LAG_SUM))
        def _():
            total(t - LAG_SUM)

        @pl.when(within(t, chunks + LAG_SUM, chunks + EARLY + LAG_SUM))
        def _():
            total_early(t - chunks - LAG_SUM)

        @pl.when(jnp.logical_and(moves, within(t, EARLY + LAG_OUT, chunks + LAG_OUT)))
        def _():
            finish(t - LAG_OUT)

        return carry

    lax.fori_loop(1, max(chunks + EARLY + LAG_SUM, chunks + LAG_OUT), body, 0)

    remote(far_s, far_r, far_ss, far_rs.at[0, 0], down).wait_send()
    remote(lo_s, hi_r, lo_ss, hi_rs.at[0], down).wait_send()
    remote(hi_s, lo_r, hi_ss, lo_rs.at[0], up).wait_send()

    @pl.when(moves)
    def _():
        remote(move_s, move_r, move_ss, move_rs.at[0], across).wait_send()
        remote(mid_s, mid_r, mid_ss, mid_rs.at[0], across).wait_send()

    pltpu.make_async_copy(o_hbm, o_hbm, o_sem).wait()


def cannon_step(shift, p_matrix, s_matrix, p_pattern, s_pattern, c_input):
    rows, depth = p_matrix.shape
    chunks = rows // CHUNK
    width = c_input.shape[1]
    plain = chunks - EARLY
    dma = pltpu.SemaphoreType.DMA
    half = lambda dtype, *lead: pltpu.VMEM((chunks, *lead, HALF, width), dtype)
    full = lambda dtype, count=chunks: pltpu.VMEM((count, CHUNK, width), dtype)
    early = pltpu.VMEM((EARLY, 3, CHUNK, width), jnp.bfloat16)
    return pl.pallas_call(
        functools.partial(kernel, shift, chunks),
        out_shape=jax.ShapeDtypeStruct(c_input.shape, jnp.float32),
        in_specs=[pl.BlockSpec(memory_space=pl.ANY)] * 5,
        out_specs=pl.BlockSpec(memory_space=pl.ANY),
        scratch_shapes=[
            pltpu.SMEM(p_pattern.shape, jnp.int32), pltpu.SMEM(s_pattern.shape, jnp.int32),
            pltpu.VMEM((chunks, CHUNK, depth), jnp.bfloat16),
            pltpu.VMEM((depth, 4 * width), jnp.bfloat16),
            full(jnp.float32), full(jnp.float32), full(jnp.float32),
            half(jnp.float32), half(jnp.float32),
            half(jnp.bfloat16, 2),
            full(jnp.bfloat16), full(jnp.bfloat16), full(jnp.bfloat16, plain), early,
            half(jnp.bfloat16, 2),
            full(jnp.bfloat16), full(jnp.bfloat16), full(jnp.bfloat16, plain), early,
            dma((2,)), dma((chunks,)), dma((4,)), dma((chunks,)), dma,
            dma, dma((chunks, 2)),
            dma, dma((chunks + 2 * EARLY,)), dma, dma((chunks + 2 * EARLY,)),
            dma, dma((plain,)), dma, dma((EARLY,)),
        ],
        compiler_params=pltpu.CompilerParams(
            collective_id=shift, has_side_effects=True, vmem_limit_bytes=56 * 2**20
        ),
        cost_estimate=pl.CostEstimate(
            flops=2 * rows * depth * 4 * width, bytes_accessed=20 * 2**20, transcendentals=0
        ),
    )(p_pattern, s_pattern, p_matrix, s_matrix, c_input)


def local(p_matrix, s_matrix, p_pattern, s_pattern, c_input, step):
    return lax.switch(
        step[0] & 3,
        [functools.partial(cannon_step, shift) for shift in range(4)],
        p_matrix, s_matrix, p_pattern.T, s_pattern, c_input,
    )


def solution(mesh):
    placed = (
        P("row", ("col", "rep")),
        P(("col", "rep"), None),
        P("row", ("col", "rep")),
        P(("col", "rep"), None),
        P("row", ("col", "rep")),
        P(),
    )
    return jax.shard_map(
        local, mesh=mesh, in_specs=placed, out_specs=P("row", ("col", "rep")), check_vma=False
    )
```
